32 devices in a mesh: seed: 2 (over x), tm: 16 (over z, y, core).
Axes of the slice: x: 2, y: 2, z: 4, core: 2. Of those that a mesh axis runs over, the one named last changes fastest.
Arguments:
- queries: bfloat16 [8192, 2560], P(('seed', 'tm')), parts along dimension 0, may hold values from -8 to 8
- keys: bfloat16 [8192, 2560], P(('seed', 'tm')), parts along dimension 0, may hold values from -6 to 6
- values: bfloat16 [8192, 2560], P(('seed', 'tm')), parts along dimension 0, may hold values from -6 to 6
- far_pick: int32 [32, 3], P('tm'), may hold values from 0 to 3
Outputs:
- attended: bfloat16 [8192, 2560], P(('seed', 'tm')), parts along dimension 0
The draws below stay inside these ranges and needn't reach their ends.
There are 2 independent parts, one for each index of `seed`. The reference program is written for one: setup_inputs(seed, part) draws one part's arguments, and reference() takes and returns one part's arrays. A program takes and returns all parts, laid end to end along the dimension named above; an argument that names none is the same for every part. Nothing has to cross between parts.
All inputs are finite; a program needn't handle non-finite values.
Results may differ from the reference program's by a relative error of at most 0.0034.
Values may be sent and summed in bfloat16 or wider, within the bound.
A program may use at most 64 MiB of HBM per device.

```python
import math
import jax
import jax.numpy as jnp
from jax import lax

H = 20
HD = 128
TILE = 128
TILES_DEV = 2
FAR_ROWS = 64
CYCLES = 3
SUBS = 4
NT = 32
TOKENS = 4096
N_TM = 16


def draw_queries(key, part):
    base = 2.0 * jnp.clip(jax.random.normal(jax.random.fold_in(key, 1), (TOKENS, H * HD), jnp.float32), -4.0, 4.0)
    return base.astype(jnp.bfloat16)


def draw_keys(key, part):
    base = jnp.clip(jax.random.normal(jax.random.fold_in(key, 2), (TOKENS, H * HD), jnp.float32), -6.0, 6.0)
    return base.astype(jnp.bfloat16)


def plant(values, key, least, largest):
    longest = values.shape.index(max(values.shape))
    spots = []
    for shift in (0, 1):
        where = [jax.random.randint(jax.random.fold_in(key, axis), (), 0, length) for axis, length in enumerate(values.shape)]
        where[longest] = (where[longest] + shift) % values.shape[longest]
        spots.append(tuple(where))
    return values.at[spots[0]].set(least).at[spots[1]].set(largest)


def shard_levels(rng, dims, split, smallest, top_value):
    loudness, own = 1.0, jax.random.fold_in(rng, 6)
    for position, parts in split:
        draws = jnp.exp(jax.random.uniform(jax.random.fold_in(own, position), (parts,), jnp.float32, smallest / len(split), top_value / len(split)))
        loudness = loudness * jnp.repeat(draws, dims[position] // parts).reshape([-1 if axis == position else 1 for axis in range(len(dims))])
    return loudness


def noise(own_key, shape, deviation, limit, pieces=(), kind=jnp.bfloat16):
    values = jax.random.normal(own_key, shape, jnp.float32) * deviation
    if len(pieces) > 0:
        values = shard_levels(own_key, shape, pieces, -0.22, 0.18) * values
    return jnp.clip(values, min=-limit, max=limit).astype(kind)


def setup_inputs(seed: int = 0, part: int = 0) -> dict:
    streams_of = jax.random.split(jax.random.key(seed), 5)
    part_splits = jax.random.split(jax.random.fold_in(streams_of[4], part), 5)
    queries = draw_queries(jax.random.fold_in(jax.random.fold_in(streams_of[4], part), 71), part)
    keys = draw_keys(jax.random.fold_in(jax.random.fold_in(streams_of[4], part), 71), part)
    values = noise(part_splits[2], (TOKENS, H * HD), 1.0, 6.0, ((0, 16),))
    far_pick = plant(jax.random.randint(streams_of[3], (NT, CYCLES), 0, SUBS), jax.random.fold_in(streams_of[3], 1), 0, SUBS - 1).astype(jnp.int32)
    return {"queries": queries, "keys": keys, "values": values, "far_pick": far_pick}


FAR_SHIFTS = (2, -4, 8)

def attend(query_tile, key_tile, value_tile, usable):
    row_count = query_tile.shape[0]
    query_heads = query_tile.reshape(row_count, H, HD).astype(jnp.float32)
    key_heads = key_tile.reshape(-1, H, HD).astype(jnp.float32)
    value_heads = value_tile.reshape(-1, H, HD).astype(jnp.float32)
    scores = jnp.einsum('qhd,khd->hqk', query_heads, key_heads) * (1.0 / math.sqrt(HD))
    scores = jnp.where(usable[None, None, :], scores, -jnp.inf)
    maxima = lax.optimization_barrier(jnp.max(scores, axis=2, keepdims=True))
    weights = jnp.exp(scores - maxima)
    totals = lax.optimization_barrier(jnp.sum(weights, axis=2))
    rounded = weights.astype(jnp.bfloat16).astype(jnp.float32)
    mixed = jnp.einsum('hqk,khd->qhd', rounded, value_heads)
    return (mixed / jnp.transpose(totals)[:, :, None]).reshape(row_count, H * HD).astype(jnp.bfloat16)

def reference(queries, keys, values, far_pick):
    token_count = queries.shape[0]
    row_dev = TILES_DEV * TILE
    tile_total = token_count // TILE

    def one_tile(tile_id):
        device = tile_id // TILES_DEV
        query_tile = lax.dynamic_slice_in_dim(queries, tile_id * TILE, TILE, 0)
        key_parts = []
        value_parts = []
        flags = []
        for step_off in (-1, 0, 1):
            other = tile_id + step_off
            inside = (other >= 0) & (other < tile_total)
            start = (jnp.clip(other, 0, tile_total - 1) * TILE).astype(jnp.int32)
            key_parts.append(lax.dynamic_slice_in_dim(keys, start, TILE, 0))
            value_parts.append(lax.dynamic_slice_in_dim(values, start, TILE, 0))
            flags.append(jnp.broadcast_to(inside, (TILE,)))
        for cycle_index, offset in enumerate(FAR_SHIFTS):
            source = device - offset
            inside = (source >= 0) & (source < N_TM)
            chosen_sub = far_pick[tile_id, cycle_index]
            start = (jnp.clip(source, 0, N_TM - 1) * row_dev + chosen_sub * FAR_ROWS).astype(jnp.int32)
            key_parts.append(lax.dynamic_slice_in_dim(keys, start, FAR_ROWS, 0))
            value_parts.append(lax.dynamic_slice_in_dim(values, start, FAR_ROWS, 0))
            flags.append(jnp.broadcast_to(inside, (FAR_ROWS,)))
        return attend(query_tile, jnp.concatenate(key_parts, 0), jnp.concatenate(value_parts, 0), jnp.concatenate(flags, 0))
    result = lax.map(one_tile, jnp.arange(tile_total, dtype=jnp.int32))
    return result.reshape(token_count, H * HD)
```

```python
import functools
import math

import jax
import jax.numpy as jnp
from jax import lax
from jax.experimental import pallas as pl
from jax.experimental.pallas import tpu as pltpu
from jax.sharding import PartitionSpec as P

HD = 128
FAR_ROWS = 64
FAR_SHIFTS = (2, -4, 8)
CYCLES = len(FAR_SHIFTS)
CHUNK = 512
PARTNERS = (8, -8, 4, -4, 2, -2, 1, -1)


def kernel(
    n, q_ref, k_ref, v_ref, pick_ref, o_ref, ext, stage, pick_in, pick_sm,
    near_send, near_recv, far_send, far_recv, pick_send, pick_recv, local_sem,
):
    me = lax.axis_index("tm")
    rows, width = q_ref.shape
    tile = rows // 2
    chunks = width // CHUNK
    heads = CHUNK // HD

    def present(other):
        return (other >= 0) & (other < n)

    for t, step in ((0, -1), (1, 1)):

        @pl.when(jnp.logical_not(present(me + step)))
        def _():
            for j in range(chunks):
                for kv in range(2):
                    ext[j, 2 * kv + t, :tile, :] = jnp.zeros((tile, CHUNK), ext.dtype)

    for c, shift in enumerate(FAR_SHIFTS):

        @pl.when(jnp.logical_not(present(me - shift)))
        def _():
            start = tile + c * FAR_ROWS
            for j in range(chunks):
                ext[j, :, start : start + FAR_ROWS, :] = jnp.zeros((4, FAR_ROWS, CHUNK), ext.dtype)

    barrier = pltpu.get_barrier_semaphore()
    count = jnp.int32(0)
    for step in PARTNERS:
        other = me + step
        ok = present(other)
        count = count + ok.astype(jnp.int32)

        @pl.when(ok)
        def _():
            pl.semaphore_signal(
                barrier, inc=1, device_id={"tm": other}, device_id_type=pl.DeviceIdType.MESH
            )

    pl.semaphore_wait(barrier, count)

    def pick_copy(c):
        return pltpu.make_async_remote_copy(
            src_ref=pick_ref, dst_ref=pick_in.at[c],
            send_sem=pick_send.at[c], recv_sem=pick_recv.at[c],
            device_id={"tm": me - FAR_SHIFTS[c]}, device_id_type=pl.DeviceIdType.MESH,
        )

    def near_copy(side, kv, j):
        source = (k_ref, v_ref)[kv]
        first = tile if side == 0 else 0
        return pltpu.make_async_remote_copy(
            src_ref=source.at[pl.ds(first, tile), pl.ds(pl.multiple_of(j * CHUNK, CHUNK), CHUNK)],
            dst_ref=ext.at[j, 2 * kv + side, pl.ds(0, tile), :],
            send_sem=near_send.at[2 * side + kv, j], recv_sem=near_recv.at[2 * side + kv, j],
            device_id={"tm": me + (1 - 2 * side)}, device_id_type=pl.DeviceIdType.MESH,
        )

    def far_copy(c, j):
        return pltpu.make_async_remote_copy(
            src_ref=stage.at[c, j],
            dst_ref=ext.at[j, :, pl.ds(tile + c * FAR_ROWS, FAR_ROWS), :],
            send_sem=far_send.at[c, j], recv_sem=far_recv.at[c, j],
            device_id={"tm": me + FAR_SHIFTS[c]}, device_id_type=pl.DeviceIdType.MESH,
        )

    for c in range(CYCLES):

        @pl.when(present(me - FAR_SHIFTS[c]))
        def _():
            pick_copy(c).start()

    for side in range(2):

        @pl.when(present(me + (1 - 2 * side)))
        def _():
            @pl.loop(0, chunks)
            def _(j):
                near_copy(side, 0, j).start()
                near_copy(side, 1, j).start()

    for c in range(CYCLES):

        @pl.when(present(me + FAR_SHIFTS[c]))
        def _():
            pick_copy(c).wait_recv()
            local = pltpu.make_async_copy(pick_in.at[c], pick_sm.at[c], local_sem.at[c])
            local.start()
            local.wait()

    @pl.loop(0, chunks)
    def _(j):
        columns = pl.ds(pl.multiple_of(j * CHUNK, CHUNK), CHUNK)
        for c in (2, 0, 1):

            @pl.when(present(me + FAR_SHIFTS[c]))
            def _():
                for t in range(2):
                    pick = pick_sm[c, 0, t * CYCLES + c]
                    for kv, source in enumerate((k_ref, v_ref)):
                        parts = [
                            source[p * FAR_ROWS : (p + 1) * FAR_ROWS, columns]
                            for p in range(rows // FAR_ROWS)
                        ]
                        chosen = parts[0]
                        for p in range(1, len(parts)):
                            chosen = jnp.where(pick == p, parts[p], chosen)
                        stage[c, j, 2 * kv + t] = chosen
                far_copy(c, j).start()

    scale = (1.0 / math.sqrt(HD)) * math.log2(math.e)
    extra = tile + CYCLES * FAR_ROWS
    place = lax.broadcasted_iota(jnp.int32, (1, extra), 1)
    biases = []
    for t in range(2):
        bias = jnp.where(present(me + (2 * t - 1)), 0.0, -jnp.inf)
        bias = jnp.full((1, extra), bias, jnp.float32)
        for c, shift in enumerate(FAR_SHIFTS):
            inside = place >= tile + c * FAR_ROWS
            bias = jnp.where(inside, jnp.where(present(me - shift), 0.0, -jnp.inf), bias)
        biases.append(bias)

    @pl.loop(0, chunks)
    def _(j):
        for side in range(2):

            @pl.when(present(me - (1 - 2 * side)))
            def _():
                near_copy(side, 0, j).wait_recv()
                near_copy(side, 1, j).wait_recv()

        for c in range(CYCLES):

            @pl.when(present(me - FAR_SHIFTS[c]))
            def _():
                far_copy(c, j).wait_recv()

        @pl.loop(0, heads)
        def _(i):
            columns = pl.ds(pl.multiple_of(j * CHUNK + i * HD, HD), HD)
            inner = pl.ds(pl.multiple_of(i * HD, HD), HD)
            own_keys = k_ref[:, columns]
            own_values = v_ref[:, columns]
            for t in range(2):
                query = q_ref[t * tile : (t + 1) * tile, columns]
                contract = (((1,), (1,)), ((), ()))
                own = lax.dot_general(query, own_keys, contract, preferred_element_type=jnp.float32)
                other = lax.dot_general(
                    query, ext[j, t, :, inner], contract, preferred_element_type=jnp.float32
                )
                other = other + biases[t]
                top = jnp.maximum(
                    jnp.max(own, axis=1, keepdims=True), jnp.max(other, axis=1, keepdims=True)
                )
                own = jnp.exp2((own - top) * scale)
                other = jnp.exp2((other - top) * scale)
                total = jnp.sum(own, axis=1, keepdims=True) + jnp.sum(other, axis=1, keepdims=True)
                mixed = jnp.dot(
                    own.astype(jnp.bfloat16), own_values, preferred_element_type=jnp.float32
                ) + jnp.dot(
                    other.astype(jnp.bfloat16), ext[j, 2 + t, :, inner],
                    preferred_element_type=jnp.float32,
                )
                o_ref[t * tile : (t + 1) * tile, columns] = (mixed / total).astype(o_ref.dtype)

    for c in range(CYCLES):

        @pl.when(present(me - FAR_SHIFTS[c]))
        def _():
            pick_copy(c).wait_send()

        @pl.when(present(me + FAR_SHIFTS[c]))
        def _():
            @pl.loop(0, chunks)
            def _(j):
                far_copy(c, j).wait_send()

    for side in range(2):

        @pl.when(present(me + (1 - 2 * side)))
        def _():
            @pl.loop(0, chunks)
            def _(j):
                near_copy(side, 0, j).wait_send()
                near_copy(side, 1, j).wait_send()


def on_device(queries, keys, values, far_pick):
    rows, width = queries.shape
    tiles = far_pick.shape[0]
    tile = rows // tiles
    chunks = width // CHUNK
    picks = jnp.pad(far_pick.reshape(1, -1), ((0, 7), (0, 128 - far_pick.size)))
    vmem = pl.BlockSpec(memory_space=pltpu.VMEM)
    dma = pltpu.SemaphoreType.DMA
    return pl.pallas_call(
        functools.partial(kernel, lax.axis_size("tm")),
        out_shape=jax.ShapeDtypeStruct((rows, width), queries.dtype),
        in_specs=[vmem] * 4,
        out_specs=vmem,
        scratch_shapes=[
            pltpu.VMEM((chunks, 2 * tiles, tile + CYCLES * FAR_ROWS, CHUNK), keys.dtype),
            pltpu.VMEM((CYCLES, chunks, 2 * tiles, FAR_ROWS, CHUNK), keys.dtype),
            pltpu.VMEM((CYCLES, 8, 128), jnp.int32),
            pltpu.SMEM((CYCLES, 8, 128), jnp.int32),
            dma((4, chunks)),
            dma((4, chunks)),
            dma((CYCLES, chunks)),
            dma((CYCLES, chunks)),
            dma((CYCLES,)),
            dma((CYCLES,)),
            dma((CYCLES,)),
        ],
        compiler_params=pltpu.CompilerParams(
            collective_id=0, has_side_effects=True, vmem_limit_bytes=48 * 2**20
        ),
    )(queries, keys, values, picks)


def solution(mesh):
    return jax.shard_map(
        on_device,
        mesh=mesh,
        in_specs=(
            P(("seed", "tm"), None),
            P(("seed", "tm"), None),
            P(("seed", "tm"), None),
            P("tm", None),
        ),
        out_specs=P(("seed", "tm"), None),
        check_vma=False,
    )
```

```python
import functools
import math

import jax
import jax.numpy as jnp
from jax import lax
from jax.experimental import pallas as pl
from jax.experimental.pallas import tpu as pltpu
from jax.sharding import PartitionSpec as P

HD = 128
FAR_ROWS = 64
FAR_SHIFTS = (2, -4, 8)
CYCLES = len(FAR_SHIFTS)
CHUNK = 512
PARTNERS = (8, -8, 4, -4, 2, -2, 1, -1)


def kernel(
    n, q_hbm, k_hbm, v_hbm, pick_ref, o_ref, q_ref, k_ref, v_ref, ext, stage, far_relay, near_relay,
    pick_in, pick_sm, near_send, near_recv, far_send, far_recv, hop_recv, on_send,
    pick_send, pick_recv, local_sem, load_sem,
):
    me = lax.axis_index("tm")
    rows, width = q_ref.shape
    loads = [
        pltpu.make_async_copy(source, target, load_sem.at[i])
        for i, (source, target) in enumerate(((k_hbm, k_ref), (v_hbm, v_ref), (q_hbm, q_ref)))
    ]
    for load in loads:
        load.start()
    tile = rows // 2
    chunks = width // CHUNK
    heads = CHUNK // HD

    def present(other):
        return (other >= 0) & (other < n)

    place4 = lax.rem(me, 4)
    far_hops = (place4 >= 2) & present(me + 2)
    far_relays = (place4 < 2) & present(me + 4)
    near_hops = (place4 == 3) & present(me + 1)
    near_relays = (place4 == 1) & present(me + 3)

    for t, step in ((0, -1), (1, 1)):

        @pl.when(jnp.logical_not(present(me + step)))
        def _():
            for j in range(chunks):
                for kv in range(2):
                    ext[j, 2 * kv + t, :tile, :] = jnp.zeros((tile, CHUNK), ext.dtype)

    for c, shift in enumerate(FAR_SHIFTS):

        @pl.when(jnp.logical_not(present(me - shift)))
        def _():
            start = tile + c * FAR_ROWS
            for j in range(chunks):
                ext[j, :, start : start + FAR_ROWS, :] = jnp.zeros((4, FAR_ROWS, CHUNK), ext.dtype)

    barrier = pltpu.get_barrier_semaphore()
    count = jnp.int32(0)
    greet = [(step, present(me + step)) for step in PARTNERS]
    greet += [(3, near_relays), (-3, (place4 == 0) & present(me - 3))]
    for step, ok in greet:
        other = me + step
        count = count + ok.astype(jnp.int32)

        @pl.when(ok)
        def _():
            pl.semaphore_signal(
                barrier, inc=1, device_id={"tm": other}, device_id_type=pl.DeviceIdType.MESH
            )

    pl.semaphore_wait(barrier, count)

    def pick_copy(c):
        return pltpu.make_async_remote_copy(
            src_ref=pick_ref, dst_ref=pick_in.at[c],
            send_sem=pick_send.at[c], recv_sem=pick_recv.at[c],
            device_id={"tm": me - FAR_SHIFTS[c]}, device_id_type=pl.DeviceIdType.MESH,
        )

    def remote(source, target, send_sem, recv_sem, step):
        return pltpu.make_async_remote_copy(
            src_ref=source, dst_ref=target, send_sem=send_sem, recv_sem=recv_sem,
            device_id={"tm": me + step}, device_id_type=pl.DeviceIdType.MESH,
        )

    def near_copy(side, kv, j, hop=False):
        source = (k_hbm, v_hbm)[kv]
        first = tile if side == 0 else 0
        columns = pl.ds(pl.multiple_of(j * CHUNK, CHUNK), CHUNK)
        source = source.at[pl.ds(first, tile), columns]
        index = 2 * side + kv
        if hop:
            return remote(source, near_relay.at[j], near_send.at[index, j], hop_recv.at[1, j], -2)
        target = ext.at[j, 2 * kv + side, pl.ds(0, tile), :]
        return remote(
            source, target, near_send.at[index, j], near_recv.at[index, j], 1 - 2 * side
        )

    def far_copy(c, j, hop=False):
        cycle, (first, count) = c % 3, {0: (0, 2), 3: (2, 2)}.get(c, (0, 4))
        source = stage.at[cycle, j, pl.ds(first, count)]
        if hop:
            return remote(source, far_relay.at[j], far_send.at[c, j], hop_recv.at[0, j], -2)
        target = ext.at[j, pl.ds(first, count), pl.ds(tile + cycle * FAR_ROWS, FAR_ROWS), :]
        return remote(source, target, far_send.at[c, j], far_recv.at[c, j], FAR_SHIFTS[cycle])

    def far_on(j):
        target = ext.at[j, pl.ds(2, 2), pl.ds(tile, FAR_ROWS), :]
        return remote(far_relay.at[j], target, on_send.at[0, j], far_recv.at[3, j], 4)

    def near_on(j):
        target = ext.at[j, 2, pl.ds(0, tile), :]
        return remote(near_relay.at[j], target, on_send.at[1, j], near_recv.at[1, j], 3)

    for c in range(CYCLES):

        @pl.when(present(me - FAR_SHIFTS[c]))
        def _():
            pick_copy(c).start()

    for side in range(2):

        @pl.when(present(me + (1 - 2 * side)))
        def _():
            @pl.loop(0, chunks)
            def _(j):
                if side == 0:

                    @pl.when(near_hops)
                    def _():
                        near_copy(0, 1, j, hop=True).start()

                    @pl.when(jnp.logical_not(near_hops))
                    def _():
                        near_copy(0, 1, j).start()

                else:
                    near_copy(1, 1, j).start()
                near_copy(side, 0, j).start()

    for c in range(CYCLES):

        @pl.when(present(me + FAR_SHIFTS[c]))
        def _():
            pick_copy(c).wait_recv()
            local = pltpu.make_async_copy(pick_in.at[c], pick_sm.at[c], local_sem.at[c])
            local.start()
            local.wait()

    loads[0].wait()
    loads[1].wait()

    @pl.loop(0, chunks)
    def _(j):
        columns = pl.ds(pl.multiple_of(j * CHUNK, CHUNK), CHUNK)
        for c in (0, 2, 1):

            @pl.when(present(me + FAR_SHIFTS[c]))
            def _():
                for t in range(2):
                    pick = pick_sm[c, 0, t * CYCLES + c]
                    for kv, source in enumerate((k_ref, v_ref)):
                        parts = [
                            source[p * FAR_ROWS : (p + 1) * FAR_ROWS, columns]
                            for p in range(rows // FAR_ROWS)
                        ]
                        chosen = parts[0]
                        for p in range(1, len(parts)):
                            chosen = jnp.where(pick == p, parts[p], chosen)
                        stage[c, j, 2 * kv + t] = chosen
                if c == 0:

                    @pl.when(far_hops)
                    def _():
                        far_copy(3, j, hop=True).start()

                    @pl.when(jnp.logical_not(far_hops))
                    def _():
                        far_copy(3, j).start()

                far_copy(c, j).start()

    @pl.when(near_relays)
    def _():
        @pl.loop(0, chunks)
        def _(j):
            near_copy(0, 1, j, hop=True).wait_recv()
            near_on(j).start()

    @pl.when(far_relays)
    def _():
        @pl.loop(0, chunks)
        def _(j):
            far_copy(3, j, hop=True).wait_recv()
            far_on(j).start()

    loads[2].wait()
    scale = (1.0 / math.sqrt(HD)) * math.log2(math.e)
    extra = tile + CYCLES * FAR_ROWS
    place = lax.broadcasted_iota(jnp.int32, (1, extra), 1)
    biases = []
    for t in range(2):
        bias = jnp.where(present(me + (2 * t - 1)), 0.0, -jnp.inf)
        bias = jnp.full((1, extra), bias, jnp.float32)
        for c, shift in enumerate(FAR_SHIFTS):
            inside = place >= tile + c * FAR_ROWS
            bias = jnp.where(inside, jnp.where(present(me - shift), 0.0, -jnp.inf), bias)
        biases.append(bias)

    @pl.loop(0, chunks)
    def _(j):
        for side in range(2):

            @pl.when(present(me - (1 - 2 * side)))
            def _():
                near_copy(side, 0, j).wait_recv()
                near_copy(side, 1, j).wait_recv()

        for c in range(CYCLES):

            @pl.when(present(me - FAR_SHIFTS[c]))
            def _():
                far_copy(c, j).wait_recv()
                if c == 0:
                    far_copy(3, j).wait_recv()

        @pl.loop(0, heads)
        def _(i):
            columns = pl.ds(pl.multiple_of(j * CHUNK + i * HD, HD), HD)
            inner = pl.ds(pl.multiple_of(i * HD, HD), HD)
            own_keys = k_ref[:, columns]
            own_values = v_ref[:, columns]
            for t in range(2):
                query = q_ref[t * tile : (t + 1) * tile, columns]
                contract = (((1,), (1,)), ((), ()))
                own = lax.dot_general(query, own_keys, contract, preferred_element_type=jnp.float32)
                other = lax.dot_general(
                    query, ext[j, t, :, inner], contract, preferred_element_type=jnp.float32
                )
                other = other + biases[t]
                top = jnp.maximum(
                    jnp.max(own, axis=1, keepdims=True), jnp.max(other, axis=1, keepdims=True)
                )
                own = jnp.exp2((own - top) * scale)
                other = jnp.exp2((other - top) * scale)
                total = jnp.sum(own, axis=1, keepdims=True) + jnp.sum(other, axis=1, keepdims=True)
                mixed = jnp.dot(
                    own.astype(jnp.bfloat16), own_values, preferred_element_type=jnp.float32
                ) + jnp.dot(
                    other.astype(jnp.bfloat16), ext[j, 2 + t, :, inner],
                    preferred_element_type=jnp.float32,
                )
                o_ref[t * tile : (t + 1) * tile, columns] = (mixed / total).astype(o_ref.dtype)

    for c in range(CYCLES):

        @pl.when(present(me - FAR_SHIFTS[c]))
        def _():
            pick_copy(c).wait_send()

        @pl.when(present(me + FAR_SHIFTS[c]))
        def _():
            @pl.loop(0, chunks)
            def _(j):
                far_copy(c, j).wait_send()
                if c == 0:
                    far_copy(3, j).wait_send()

    for side in range(2):

        @pl.when(present(me + (1 - 2 * side)))
        def _():
            @pl.loop(0, chunks)
            def _(j):
                near_copy(side, 0, j).wait_send()
                near_copy(side, 1, j).wait_send()

    @pl.when(near_relays)
    def _():
        @pl.loop(0, chunks)
        def _(j):
            near_on(j).wait_send()

    @pl.when(far_relays)
    def _():
        @pl.loop(0, chunks)
        def _(j):
            far_on(j).wait_send()


def on_device(queries, keys, values, far_pick):
    rows, width = queries.shape
    tiles = far_pick.shape[0]
    tile = rows // tiles
    chunks = width // CHUNK
    picks = jnp.pad(far_pick.reshape(1, -1), ((0, 7), (0, 128 - far_pick.size)))
    vmem = pl.BlockSpec(memory_space=pltpu.VMEM)
    hbm = pl.BlockSpec(memory_space=pl.ANY)
    dma = pltpu.SemaphoreType.DMA
    return pl.pallas_call(
        functools.partial(kernel, lax.axis_size("tm")),
        out_shape=jax.ShapeDtypeStruct((rows, width), queries.dtype),
        in_specs=[hbm] * 3 + [vmem],
        out_specs=vmem,
        scratch_shapes=[
            pltpu.VMEM((rows, width), queries.dtype),
            pltpu.VMEM((rows, width), keys.dtype),
            pltpu.VMEM((rows, width), values.dtype),
            pltpu.VMEM((chunks, 2 * tiles, tile + CYCLES * FAR_ROWS, CHUNK), keys.dtype),
            pltpu.VMEM((CYCLES, chunks, 2 * tiles, FAR_ROWS, CHUNK), keys.dtype),
            pltpu.VMEM((chunks, tiles, FAR_ROWS, CHUNK), values.dtype),
            pltpu.VMEM((chunks, tile, CHUNK), values.dtype),
            pltpu.VMEM((CYCLES, 8, 128), jnp.int32),
            pltpu.SMEM((CYCLES, 8, 128), jnp.int32),
            dma((4, chunks)),
            dma((4, chunks)),
            dma((CYCLES + 1, chunks)),
            dma((CYCLES + 1, chunks)),
            dma((2, chunks)),
            dma((2, chunks)),
            dma((CYCLES,)),
            dma((CYCLES,)),
            dma((CYCLES,)),
            dma((3,)),
        ],
        compiler_params=pltpu.CompilerParams(
            collective_id=0, has_side_effects=True, vmem_limit_bytes=56 * 2**20
        ),
    )(queries, keys, values, picks)


def solution(mesh):
    return jax.shard_map(
        on_device,
        mesh=mesh,
        in_specs=(
            P(("seed", "tm"), None),
            P(("seed", "tm"), None),
            P(("seed", "tm"), None),
            P("tm", None),
        ),
        out_specs=P(("seed", "tm"), None),
        check_vma=False,
    )
```

```python
import functools
import math

import jax
import jax.numpy as jnp
from jax import lax
from jax.experimental import pallas as pl
from jax.experimental.pallas import tpu as pltpu
from jax.sharding import PartitionSpec as P

HD = 128
FAR_ROWS = 64
FAR_SHIFTS = (2, -4, 8)
CYCLES = len(FAR_SHIFTS)
CHUNK = 512
PARTNERS = (8, -8, 4, -4, 2, -2, 1, -1)


def kernel(
    n, q_hbm, k_hbm, v_hbm, pick_ref, o_ref, q_ref, k_ref, v_ref, ext, stage, far_relay, near_relay,
    pick_in, pick_sm, near_send, near_recv, far_send, far_recv, hop_recv, on_send,
    pick_send, pick_recv, local_sem, load_sem,
):
    me = lax.axis_index("tm")
    rows, width = q_ref.shape
    loads = [
        pltpu.make_async_copy(source, target, load_sem.at[i])
        for i, (source, target) in enumerate(((k_hbm, k_ref), (v_hbm, v_ref), (q_hbm, q_ref)))
    ]
    for load in loads:
        load.start()
    tile = rows // 2
    chunks = width // CHUNK
    heads = CHUNK // HD

    def present(other):
        return (other >= 0) & (other < n)

    place4 = lax.rem(me, 4)
    far_hops = (place4 >= 2) & present(me + 2)
    far_relays = (place4 < 2) & present(me + 4)
    near_hops = (place4 == 3) & present(me + 1)
    near_relays = (place4 == 1) & present(me + 3)

    for t, step in ((0, -1), (1, 1)):

        @pl.when(jnp.logical_not(present(me + step)))
        def _():
            for j in range(chunks):
                for kv in range(2):
                    ext[j, 2 * kv + t, :tile, :] = jnp.zeros((tile, CHUNK), ext.dtype)

    for c, shift in enumerate(FAR_SHIFTS):

        @pl.when(jnp.logical_not(present(me - shift)))
        def _():
            start = tile + c * FAR_ROWS
            for j in range(chunks):
                ext[j, :, start : start + FAR_ROWS, :] = jnp.zeros((4, FAR_ROWS, CHUNK), ext.dtype)

    barrier = pltpu.get_barrier_semaphore()
    count = jnp.int32(0)
    greet = [(step, present(me + step)) for step in PARTNERS]
    greet += [(3, near_relays), (-3, (place4 == 0) & present(me - 3))]
    for step, ok in greet:
        other = me + step
        count = count + ok.astype(jnp.int32)

        @pl.when(ok)
        def _():
            pl.semaphore_signal(
                barrier, inc=1, device_id={"tm": other}, device_id_type=pl.DeviceIdType.MESH
            )

    pl.semaphore_wait(barrier, count)

    def pick_copy(c):
        return pltpu.make_async_remote_copy(
            src_ref=pick_ref, dst_ref=pick_in.at[c],
            send_sem=pick_send.at[c], recv_sem=pick_recv.at[c],
            device_id={"tm": me - FAR_SHIFTS[c]}, device_id_type=pl.DeviceIdType.MESH,
        )

    def remote(source, target, send_sem, recv_sem, step):
        return pltpu.make_async_remote_copy(
            src_ref=source, dst_ref=target, send_sem=send_sem, recv_sem=recv_sem,
            device_id={"tm": me + step}, device_id_type=pl.DeviceIdType.MESH,
        )

    def near_copy(side, kv, j, hop=False):
        source = (k_hbm, v_hbm)[kv]
        first = tile if side == 0 else 0
        columns = pl.ds(pl.multiple_of(j * CHUNK, CHUNK), CHUNK)
        source = source.at[pl.ds(first, tile), columns]
        index = 2 * side + kv
        if hop:
            return remote(source, near_relay.at[j], near_send.at[index, j], hop_recv.at[1, j], -2)
        target = ext.at[j, 2 * kv + side, pl.ds(0, tile), :]
        return remote(
            source, target, near_send.at[index, j], near_recv.at[index, j], 1 - 2 * side
        )

    def far_copy(c, j, hop=False):
        cycle, (first, count) = c % 3, {0: (0, 2), 3: (2, 2)}.get(c, (0, 4))
        source = stage.at[cycle, j, pl.ds(first, count)]
        if hop:
            return remote(source, far_relay.at[j], far_send.at[c, j], hop_recv.at[0, j], -2)
        target = ext.at[j, pl.ds(first, count), pl.ds(tile + cycle * FAR_ROWS, FAR_ROWS), :]
        return remote(source, target, far_send.at[c, j], far_recv.at[c, j], FAR_SHIFTS[cycle])

    def far_on(j):
        target = ext.at[j, pl.ds(2, 2), pl.ds(tile, FAR_ROWS), :]
        return remote(far_relay.at[j], target, on_send.at[0, j], far_recv.at[3, j], 4)

    def near_on(j):
        target = ext.at[j, 2, pl.ds(0, tile), :]
        return remote(near_relay.at[j], target, on_send.at[1, j], near_recv.at[1, j], 3)

    for c in range(CYCLES):

        @pl.when(present(me - FAR_SHIFTS[c]))
        def _():
            pick_copy(c).start()

    def send_near(j):
        @pl.when(present(me + 1))
        def _():
            near_copy(0, 0, j).start()

            @pl.when(jnp.logical_not(near_hops))
            def _():
                near_copy(0, 1, j).start()

        @pl.when(present(me - 1))
        def _():
            near_copy(1, 0, j).start()
            near_copy(1, 1, j).start()

    def fill(c, j):
        columns = pl.ds(pl.multiple_of(j * CHUNK, CHUNK), CHUNK)
        for t in range(2):
            pick = pick_sm[c, 0, t * CYCLES + c]
            for kv, source in enumerate((k_ref, v_ref)):
                chosen = source[:FAR_ROWS, columns]
                for p in range(1, rows // FAR_ROWS):
                    part = source[p * FAR_ROWS : (p + 1) * FAR_ROWS, columns]
                    chosen = jnp.where(pick == p, part, chosen)
                stage[c, j, 2 * kv + t] = chosen

    def send_far(c, j):
        @pl.when(present(me + FAR_SHIFTS[c]))
        def _():
            fill(c, j)
            far_copy(c, j).start()

    for c in range(CYCLES):

        @pl.when(present(me + FAR_SHIFTS[c]))
        def _():
            pick_copy(c).wait_recv()
            local = pltpu.make_async_copy(pick_in.at[c], pick_sm.at[c], local_sem.at[c])
            local.start()
            local.wait()

    loads[0].wait()
    loads[1].wait()
    send_far(2, 0)

    @pl.when(present(me + 2))
    def _():
        @pl.loop(0, chunks)
        def _(j):
            fill(0, j)

            @pl.when(far_hops)
            def _():
                far_copy(3, j, hop=True).start()

            @pl.when(near_hops)
            def _():
                near_copy(0, 1, j, hop=True).start()

    @pl.when(near_hops & jnp.logical_not(present(me + 2)))
    def _():
        @pl.loop(0, chunks)
        def _(j):
            near_copy(0, 1, j, hop=True).start()

    @pl.loop(0, chunks)
    def _(j):
        @pl.when(j + 1 < chunks)
        def _():
            send_far(2, j + 1)

        @pl.when(present(me + 2))
        def _():
            far_copy(0, j).start()

            @pl.when(jnp.logical_not(far_hops))
            def _():
                far_copy(3, j).start()

        send_far(1, j)

        @pl.when(far_relays)
        def _():
            far_copy(3, j, hop=True).wait_recv()
            far_on(j).start()

        @pl.when(near_relays)
        def _():
            near_copy(0, 1, j, hop=True).wait_recv()
            near_on(j).start()

        send_near(j)

    loads[2].wait()
    scale = (1.0 / math.sqrt(HD)) * math.log2(math.e)
    extra = tile + CYCLES * FAR_ROWS
    place = lax.broadcasted_iota(jnp.int32, (1, extra), 1)
    biases = []
    for t in range(2):
        bias = jnp.where(present(me + (2 * t - 1)), 0.0, -jnp.inf)
        bias = jnp.full((1, extra), bias, jnp.float32)
        for c, shift in enumerate(FAR_SHIFTS):
            inside = place >= tile + c * FAR_ROWS
            bias = jnp.where(inside, jnp.where(present(me - shift), 0.0, -jnp.inf), bias)
        biases.append(bias)

    @pl.loop(0, chunks)
    def _(j):
        for side in range(2):

            @pl.when(present(me - (1 - 2 * side)))
            def _():
                near_copy(side, 0, j).wait_recv()
                near_copy(side, 1, j).wait_recv()

        for c in range(CYCLES):

            @pl.when(present(me - FAR_SHIFTS[c]))
            def _():
                far_copy(c, j).wait_recv()
                if c == 0:
                    far_copy(3, j).wait_recv()

        @pl.loop(0, heads)
        def _(i):
            columns = pl.ds(pl.multiple_of(j * CHUNK + i * HD, HD), HD)
            inner = pl.ds(pl.multiple_of(i * HD, HD), HD)
            own_keys = k_ref[:, columns]
            own_values = v_ref[:, columns]
            for t in range(2):
                query = q_ref[t * tile : (t + 1) * tile, columns]
                contract = (((1,), (1,)), ((), ()))
                own = lax.dot_general(query, own_keys, contract, preferred_element_type=jnp.float32)
                other = lax.dot_general(
                    query, ext[j, t, :, inner], contract, preferred_element_type=jnp.float32
                )
                other = other + biases[t]
                top = jnp.maximum(
                    jnp.max(own, axis=1, keepdims=True), jnp.max(other, axis=1, keepdims=True)
                )
                own = jnp.exp2((own - top) * scale)
                other = jnp.exp2((other - top) * scale)
                total = jnp.sum(own, axis=1, keepdims=True) + jnp.sum(other, axis=1, keepdims=True)
                mixed = jnp.dot(
                    own.astype(jnp.bfloat16), own_values, preferred_element_type=jnp.float32
                ) + jnp.dot(
                    other.astype(jnp.bfloat16), ext[j, 2 + t, :, inner],
                    preferred_element_type=jnp.float32,
                )
                o_ref[t * tile : (t + 1) * tile, columns] = (mixed / total).astype(o_ref.dtype)

    for c in range(CYCLES):

        @pl.when(present(me - FAR_SHIFTS[c]))
        def _():
            pick_copy(c).wait_send()

        @pl.when(present(me + FAR_SHIFTS[c]))
        def _():
            @pl.loop(0, chunks)
            def _(j):
                far_copy(c, j).wait_send()
                if c == 0:
                    far_copy(3, j).wait_send()

    for side in range(2):

        @pl.when(present(me + (1 - 2 * side)))
        def _():
            @pl.loop(0, chunks)
            def _(j):
                near_copy(side, 0, j).wait_send()
                near_copy(side, 1, j).wait_send()

    @pl.when(near_relays)
    def _():
        @pl.loop(0, chunks)
        def _(j):
            near_on(j).wait_send()

    @pl.when(far_relays)
    def _():
        @pl.loop(0, chunks)
        def _(j):
            far_on(j).wait_send()


def on_device(queries, keys, values, far_pick):
    rows, width = queries.shape
    tiles = far_pick.shape[0]
    tile = rows // tiles
    chunks = width // CHUNK
    picks = jnp.pad(far_pick.reshape(1, -1), ((0, 7), (0, 128 - far_pick.size)))
    vmem = pl.BlockSpec(memory_space=pltpu.VMEM)
    hbm = pl.BlockSpec(memory_space=pl.ANY)
    dma = pltpu.SemaphoreType.DMA
    return pl.pallas_call(
        functools.partial(kernel, lax.axis_size("tm")),
        out_shape=jax.ShapeDtypeStruct((rows, width), queries.dtype),
        in_specs=[hbm] * 3 + [vmem],
        out_specs=vmem,
        scratch_shapes=[
            pltpu.VMEM((rows, width), queries.dtype),
            pltpu.VMEM((rows, width), keys.dtype),
            pltpu.VMEM((rows, width), values.dtype),
            pltpu.VMEM((chunks, 2 * tiles, tile + CYCLES * FAR_ROWS, CHUNK), keys.dtype),
            pltpu.VMEM((CYCLES, chunks, 2 * tiles, FAR_ROWS, CHUNK), keys.dtype),
            pltpu.VMEM((chunks, tiles, FAR_ROWS, CHUNK), values.dtype),
            pltpu.VMEM((chunks, tile, CHUNK), values.dtype),
            pltpu.VMEM((CYCLES, 8, 128), jnp.int32),
            pltpu.SMEM((CYCLES, 8, 128), jnp.int32),
            dma((4, chunks)),
            dma((4, chunks)),
            dma((CYCLES + 1, chunks)),
            dma((CYCLES + 1, chunks)),
            dma((2, chunks)),
            dma((2, chunks)),
            dma((CYCLES,)),
            dma((CYCLES,)),
            dma((CYCLES,)),
            dma((3,)),
        ],
        compiler_params=pltpu.CompilerParams(
            collective_id=0, has_side_effects=True, vmem_limit_bytes=56 * 2**20
        ),
    )(queries, keys, values, picks)


def solution(mesh):
    return jax.shard_map(
        on_device,
        mesh=mesh,
        in_specs=(
            P(("seed", "tm"), None),
            P(("seed", "tm"), None),
            P(("seed", "tm"), None),
            P("tm", None),
        ),
        out_specs=P(("seed", "tm"), None),
        check_vma=False,
    )
```

```python
import functools
import math

import jax
import jax.numpy as jnp
from jax import lax
from jax.experimental import pallas as pl
from jax.experimental.pallas import tpu as pltpu
from jax.sharding import PartitionSpec as P

HD = 128
FAR_ROWS = 64
FAR_SHIFTS = (2, -4, 8)
CYCLES = len(FAR_SHIFTS)
CHUNK = 256
AHEAD = 2
PARTNERS = (8, -8, 4, -4, 2, -2, 1, -1)


def kernel(
    n, q_hbm, k_hbm, v_hbm, pick_ref, o_ref, q_ref, k_ref, v_ref, ext, stage, far_relay, near_relay,
    pick_in, pick_sm, near_send, near_recv, far_send, far_recv, hop_recv, on_send,
    pick_send, pick_recv, local_sem, load_sem,
):
    me = lax.axis_index("tm")
    rows, width = q_ref.shape
    loads = [
        pltpu.make_async_copy(source, target, load_sem.at[i])
        for i, (source, target) in enumerate(((k_hbm, k_ref), (v_hbm, v_ref), (q_hbm, q_ref)))
    ]
    for load in loads:
        load.start()
    tile = rows // 2
    chunks = width // CHUNK
    heads = CHUNK // HD

    def present(other):
        return (other >= 0) & (other < n)

    place4 = lax.rem(me, 4)
    far_hops = (place4 >= 2) & present(me + 2)
    far_relays = (place4 < 2) & present(me + 4)
    near_hops = (place4 == 3) & present(me + 1)
    near_relays = (place4 == 1) & present(me + 3)

    for t, step in ((0, -1), (1, 1)):

        @pl.when(jnp.logical_not(present(me + step)))
        def _():
            for j in range(chunks):
                for kv in range(2):
                    ext[j, 2 * kv + t, :tile, :] = jnp.zeros((tile, CHUNK), ext.dtype)

    for c, shift in enumerate(FAR_SHIFTS):

        @pl.when(jnp.logical_not(present(me - shift)))
        def _():
            start = tile + c * FAR_ROWS
            for j in range(chunks):
                ext[j, :, start : start + FAR_ROWS, :] = jnp.zeros((4, FAR_ROWS, CHUNK), ext.dtype)

    barrier = pltpu.get_barrier_semaphore()
    count = jnp.int32(0)
    greet = [(step, present(me + step)) for step in PARTNERS]
    greet += [(3, near_relays), (-3, (place4 == 0) & present(me - 3))]
    for step, ok in greet:
        other = me + step
        count = count + ok.astype(jnp.int32)

        @pl.when(ok)
        def _():
            pl.semaphore_signal(
                barrier, inc=1, device_id={"tm": other}, device_id_type=pl.DeviceIdType.MESH
            )

    pl.semaphore_wait(barrier, count)

    def pick_copy(c):
        return pltpu.make_async_remote_copy(
            src_ref=pick_ref, dst_ref=pick_in.at[c],
            send_sem=pick_send.at[c], recv_sem=pick_recv.at[c],
            device_id={"tm": me - FAR_SHIFTS[c]}, device_id_type=pl.DeviceIdType.MESH,
        )

    def remote(source, target, send_sem, recv_sem, step):
        return pltpu.make_async_remote_copy(
            src_ref=source, dst_ref=target, send_sem=send_sem, recv_sem=recv_sem,
            device_id={"tm": me + step}, device_id_type=pl.DeviceIdType.MESH,
        )

    def near_copy(side, kv, j, hop=False):
        source = (k_hbm, v_hbm)[kv]
        first = tile if side == 0 else 0
        columns = pl.ds(pl.multiple_of(j * CHUNK, CHUNK), CHUNK)
        source = source.at[pl.ds(first, tile), columns]
        index = 2 * side + kv
        if hop:
            return remote(source, near_relay.at[j], near_send.at[index, j], hop_recv.at[1, j], -2)
        target = ext.at[j, 2 * kv + side, pl.ds(0, tile), :]
        return remote(
            source, target, near_send.at[index, j], near_recv.at[index, j], 1 - 2 * side
        )

    def far_copy(c, j, hop=False):
        cycle, (first, count) = c % 3, {0: (0, 2), 3: (2, 2)}.get(c, (0, 4))
        source = stage.at[cycle, j, pl.ds(first, count)]
        if hop:
            return remote(source, far_relay.at[j], far_send.at[c, j], hop_recv.at[0, j], -2)
        target = ext.at[j, pl.ds(first, count), pl.ds(tile + cycle * FAR_ROWS, FAR_ROWS), :]
        return remote(source, target, far_send.at[c, j], far_recv.at[c, j], FAR_SHIFTS[cycle])

    def far_on(j):
        target = ext.at[j, pl.ds(2, 2), pl.ds(tile, FAR_ROWS), :]
        return remote(far_relay.at[j], target, on_send.at[0, j], far_recv.at[3, j], 4)

    def near_on(j):
        target = ext.at[j, 2, pl.ds(0, tile), :]
        return remote(near_relay.at[j], target, on_send.at[1, j], near_recv.at[1, j], 3)

    for c in range(CYCLES):

        @pl.when(present(me - FAR_SHIFTS[c]))
        def _():
            pick_copy(c).start()

    def send_near(j):
        @pl.when(present(me + 1) & (place4 != 3))
        def _():
            near_copy(0, 0, j).start()
            near_copy(0, 1, j).start()

        @pl.when(present(me - 1))
        def _():
            near_copy(1, 0, j).start()
            near_copy(1, 1, j).start()

    def fill(c, j):
        columns = pl.ds(pl.multiple_of(j * CHUNK, CHUNK), CHUNK)
        for t in range(2):
            pick = pick_sm[c, 0, t * CYCLES + c]
            for kv, source in enumerate((k_ref, v_ref)):
                chosen = source[:FAR_ROWS, columns]
                for p in range(1, rows // FAR_ROWS):
                    part = source[p * FAR_ROWS : (p + 1) * FAR_ROWS, columns]
                    chosen = jnp.where(pick == p, part, chosen)
                stage[c, j, 2 * kv + t] = chosen

    def send_far(c, j):
        @pl.when(present(me + FAR_SHIFTS[c]))
        def _():
            fill(c, j)
            far_copy(c, j).start()

    @pl.when(near_hops)
    def _():
        @pl.loop(0, chunks)
        def _(j):
            near_copy(0, 1, j, hop=True).start()
            near_copy(0, 0, j).start()

    for c in range(CYCLES):

        @pl.when(present(me + FAR_SHIFTS[c]))
        def _():
            pick_copy(c).wait_recv()
            local = pltpu.make_async_copy(pick_in.at[c], pick_sm.at[c], local_sem.at[c])
            local.start()
            local.wait()

    loads[0].wait()
    loads[1].wait()
    for j in range(AHEAD):
        send_far(2, j)

    @pl.when(present(me + 2))
    def _():
        @pl.loop(0, chunks)
        def _(j):
            fill(0, j)

            @pl.when(far_hops)
            def _():
                far_copy(3, j, hop=True).start()

    @pl.loop(0, chunks)
    def _(j):
        @pl.when(near_relays)
        def _():
            near_copy(0, 1, j, hop=True).wait_recv()
            near_on(j).start()

        @pl.when(far_relays)
        def _():
            far_copy(3, j, hop=True).wait_recv()
            far_on(j).start()

        @pl.when(j + AHEAD < chunks)
        def _():
            send_far(2, j + AHEAD)

        @pl.when(present(me + 2))
        def _():
            far_copy(0, j).start()

            @pl.when(jnp.logical_not(far_hops))
            def _():
                far_copy(3, j).start()

        send_far(1, j)
        send_near(j)

    loads[2].wait()
    scale = (1.0 / math.sqrt(HD)) * math.log2(math.e)
    extra = tile + CYCLES * FAR_ROWS
    place = lax.broadcasted_iota(jnp.int32, (1, extra), 1)
    biases = []
    for t in range(2):
        bias = jnp.where(present(me + (2 * t - 1)), 0.0, -jnp.inf)
        bias = jnp.full((1, extra), bias, jnp.float32)
        for c, shift in enumerate(FAR_SHIFTS):
            inside = place >= tile + c * FAR_ROWS
            bias = jnp.where(inside, jnp.where(present(me - shift), 0.0, -jnp.inf), bias)
        biases.append(bias)

    @pl.loop(0, chunks)
    def _(j):
        for side in range(2):

            @pl.when(present(me - (1 - 2 * side)))
            def _():
                near_copy(side, 0, j).wait_recv()
                near_copy(side, 1, j).wait_recv()

        for c in range(CYCLES):

            @pl.when(present(me - FAR_SHIFTS[c]))
            def _():
                far_copy(c, j).wait_recv()
                if c == 0:
                    far_copy(3, j).wait_recv()

        @pl.loop(0, heads)
        def _(i):
            columns = pl.ds(pl.multiple_of(j * CHUNK + i * HD, HD), HD)
            inner = pl.ds(pl.multiple_of(i * HD, HD), HD)
            own_keys = k_ref[:, columns]
            own_values = v_ref[:, columns]
            for t in range(2):
                query = q_ref[t * tile : (t + 1) * tile, columns]
                contract = (((1,), (1,)), ((), ()))
                own = lax.dot_general(query, own_keys, contract, preferred_element_type=jnp.float32)
                other = lax.dot_general(
                    query, ext[j, t, :, inner], contract, preferred_element_type=jnp.float32
                )
                other = other + biases[t]
                top = jnp.maximum(
                    jnp.max(own, axis=1, keepdims=True), jnp.max(other, axis=1, keepdims=True)
                )
                own = jnp.exp2((own - top) * scale)
                other = jnp.exp2((other - top) * scale)
                total = jnp.sum(own, axis=1, keepdims=True) + jnp.sum(other, axis=1, keepdims=True)
                mixed = jnp.dot(
                    own.astype(jnp.bfloat16), own_values, preferred_element_type=jnp.float32
                ) + jnp.dot(
                    other.astype(jnp.bfloat16), ext[j, 2 + t, :, inner],
                    preferred_element_type=jnp.float32,
                )
                o_ref[t * tile : (t + 1) * tile, columns] = (mixed / total).astype(o_ref.dtype)

    for c in range(CYCLES):

        @pl.when(present(me - FAR_SHIFTS[c]))
        def _():
            pick_copy(c).wait_send()

        @pl.when(present(me + FAR_SHIFTS[c]))
        def _():
            @pl.loop(0, chunks)
            def _(j):
                far_copy(c, j).wait_send()
                if c == 0:
                    far_copy(3, j).wait_send()

    for side in range(2):

        @pl.when(present(me + (1 - 2 * side)))
        def _():
            @pl.loop(0, chunks)
            def _(j):
                near_copy(side, 0, j).wait_send()
                near_copy(side, 1, j).wait_send()

    @pl.when(near_relays)
    def _():
        @pl.loop(0, chunks)
        def _(j):
            near_on(j).wait_send()

    @pl.when(far_relays)
    def _():
        @pl.loop(0, chunks)
        def _(j):
            far_on(j).wait_send()


def on_device(queries, keys, values, far_pick):
    rows, width = queries.shape
    tiles = far_pick.shape[0]
    tile = rows // tiles
    chunks = width // CHUNK
    picks = jnp.pad(far_pick.reshape(1, -1), ((0, 7), (0, 128 - far_pick.size)))
    vmem = pl.BlockSpec(memory_space=pltpu.VMEM)
    hbm = pl.BlockSpec(memory_space=pltpu.HBM)
    dma = pltpu.SemaphoreType.DMA
    return pl.pallas_call(
        functools.partial(kernel, lax.axis_size("tm")),
        out_shape=jax.ShapeDtypeStruct((rows, width), queries.dtype),
        in_specs=[hbm] * 3 + [vmem],
        out_specs=vmem,
        scratch_shapes=[
            pltpu.VMEM((rows, width), queries.dtype),
            pltpu.VMEM((rows, width), keys.dtype),
            pltpu.VMEM((rows, width), values.dtype),
            pltpu.VMEM((chunks, 2 * tiles, tile + CYCLES * FAR_ROWS, CHUNK), keys.dtype),
            pltpu.VMEM((CYCLES, chunks, 2 * tiles, FAR_ROWS, CHUNK), keys.dtype),
            pltpu.VMEM((chunks, tiles, FAR_ROWS, CHUNK), values.dtype),
            pltpu.VMEM((chunks, tile, CHUNK), values.dtype),
            pltpu.VMEM((CYCLES, 8, 128), jnp.int32),
            pltpu.SMEM((CYCLES, 8, 128), jnp.int32),
            dma((4, chunks)),
            dma((4, chunks)),
            dma((CYCLES + 1, chunks)),
            dma((CYCLES + 1, chunks)),
            dma((2, chunks)),
            dma((2, chunks)),
            dma((CYCLES,)),
            dma((CYCLES,)),
            dma((CYCLES,)),
            dma((3,)),
        ],
        compiler_params=pltpu.CompilerParams(
            collective_id=0, has_side_effects=True, vmem_limit_bytes=24 * 2**20
        ),
    )(queries, keys, values, picks)


def solution(mesh):
    return jax.shard_map(
        on_device,
        mesh=mesh,
        in_specs=(
            P(("seed", "tm"), None),
            P(("seed", "tm"), None),
            P(("seed", "tm"), None),
            P("tm", None),
        ),
        out_specs=P(("seed", "tm"), None),
        check_vma=False,
    )
```

```python
import functools
import math

import jax
import jax.numpy as jnp
from jax import lax
from jax.experimental import pallas as pl
from jax.experimental.pallas import tpu as pltpu
from jax.sharding import PartitionSpec as P

HD = 128
FAR_ROWS = 64
FAR_SHIFTS = (2, -4, 8)
CYCLES = len(FAR_SHIFTS)
CHUNK = 256
AHEAD = 2
PARTNERS = (8, -8, 4, -4, 2, -2, 1, -1)


def kernel(
    n, q_hbm, k_hbm, v_hbm, pick_ref, o_ref, q_ref, k_ref, v_ref, ext, stage, far_relay, near_relay,
    pick_in, pick_sm, near_send, near_recv, far_send, far_recv, hop_recv, on_send,
    pick_send, pick_recv, local_sem, load_sem,
):
    me = lax.axis_index("tm")
    rows, width = q_ref.shape
    loads = [
        pltpu.make_async_copy(source, target, load_sem.at[i])
        for i, (source, target) in enumerate(((k_hbm, k_ref), (v_hbm, v_ref), (q_hbm, q_ref)))
    ]
    for load in loads:
        load.start()
    tile = rows // 2
    chunks = width // CHUNK
    heads = CHUNK // HD
    near_hop_chunks = chunks * 7 // 10

    def present(other):
        return (other >= 0) & (other < n)

    place4 = lax.rem(me, 4)
    far_hops = (place4 >= 2) & present(me + 2)
    far_relays = (place4 < 2) & present(me + 4)
    near_hops = (place4 == 3) & present(me + 1)
    near_relays = (place4 == 1) & present(me + 3)

    for t, step in ((0, -1), (1, 1)):

        @pl.when(jnp.logical_not(present(me + step)))
        def _():
            for j in range(chunks):
                for kv in range(2):
                    ext[j, 2 * kv + t, :tile, :] = jnp.zeros((tile, CHUNK), ext.dtype)

    for c, shift in enumerate(FAR_SHIFTS):

        @pl.when(jnp.logical_not(present(me - shift)))
        def _():
            start = tile + c * FAR_ROWS
            for j in range(chunks):
                ext[j, :, start : start + FAR_ROWS, :] = jnp.zeros((4, FAR_ROWS, CHUNK), ext.dtype)

    barrier = pltpu.get_barrier_semaphore()
    count = jnp.int32(0)
    greet = [(step, present(me + step)) for step in PARTNERS]
    greet += [(3, near_relays), (-3, (place4 == 0) & present(me - 3))]
    for step, ok in greet:
        other = me + step
        count = count + ok.astype(jnp.int32)

        @pl.when(ok)
        def _():
            pl.semaphore_signal(
                barrier, inc=1, device_id={"tm": other}, device_id_type=pl.DeviceIdType.MESH
            )

    pl.semaphore_wait(barrier, count)

    def pick_copy(c):
        return pltpu.make_async_remote_copy(
            src_ref=pick_ref, dst_ref=pick_in.at[c],
            send_sem=pick_send.at[c], recv_sem=pick_recv.at[c],
            device_id={"tm": me - FAR_SHIFTS[c]}, device_id_type=pl.DeviceIdType.MESH,
        )

    def remote(source, target, send_sem, recv_sem, step):
        return pltpu.make_async_remote_copy(
            src_ref=source, dst_ref=target, send_sem=send_sem, recv_sem=recv_sem,
            device_id={"tm": me + step}, device_id_type=pl.DeviceIdType.MESH,
        )

    def near_copy(side, kv, j, hop=False):
        source = (k_hbm, v_hbm)[kv]
        first = tile if side == 0 else 0
        columns = pl.ds(pl.multiple_of(j * CHUNK, CHUNK), CHUNK)
        source = source.at[pl.ds(first, tile), columns]
        index = 2 * side + kv
        if hop:
            return remote(source, near_relay.at[j], near_send.at[index, j], hop_recv.at[1, j], -2)
        target = ext.at[j, 2 * kv + side, pl.ds(0, tile), :]
        return remote(
            source, target, near_send.at[index, j], near_recv.at[index, j], 1 - 2 * side
        )

    def far_copy(c, j, hop=False):
        cycle, (first, count) = c % 3, {0: (0, 2), 3: (2, 2)}.get(c, (0, 4))
        source = stage.at[cycle, j, pl.ds(first, count)]
        if hop:
            return remote(source, far_relay.at[j], far_send.at[c, j], hop_recv.at[0, j], -2)
        target = ext.at[j, pl.ds(first, count), pl.ds(tile + cycle * FAR_ROWS, FAR_ROWS), :]
        return remote(source, target, far_send.at[c, j], far_recv.at[c, j], FAR_SHIFTS[cycle])

    def far_on(j):
        target = ext.at[j, pl.ds(2, 2), pl.ds(tile, FAR_ROWS), :]
        return remote(far_relay.at[j], target, on_send.at[0, j], far_recv.at[3, j], 4)

    def near_on(j):
        target = ext.at[j, 2, pl.ds(0, tile), :]
        return remote(near_relay.at[j], target, on_send.at[1, j], near_recv.at[1, j], 3)

    for c in range(CYCLES):

        @pl.when(present(me - FAR_SHIFTS[c]))
        def _():
            pick_copy(c).start()

    def send_near(j):
        @pl.when(present(me + 1) & (place4 != 3))
        def _():
            near_copy(0, 0, j).start()
            near_copy(0, 1, j).start()

        @pl.when(present(me - 1))
        def _():
            near_copy(1, 0, j).start()
            near_copy(1, 1, j).start()

    def fill(c, j):
        columns = pl.ds(pl.multiple_of(j * CHUNK, CHUNK), CHUNK)
        for t in range(2):
            pick = pick_sm[c, 0, t * CYCLES + c]
            for kv, source in enumerate((k_ref, v_ref)):
                chosen = source[:FAR_ROWS, columns]
                for p in range(1, rows // FAR_ROWS):
                    part = source[p * FAR_ROWS : (p + 1) * FAR_ROWS, columns]
                    chosen = jnp.where(pick == p, part, chosen)
                stage[c, j, 2 * kv + t] = chosen

    def send_far(c, j):
        @pl.when(present(me + FAR_SHIFTS[c]))
        def _():
            fill(c, j)
            far_copy(c, j).start()

    @pl.when(near_hops)
    def _():
        @pl.loop(0, chunks)
        def _(j):
            @pl.when(j < near_hop_chunks)
            def _():
                near_copy(0, 1, j, hop=True).start()

            @pl.when(j >= near_hop_chunks)
            def _():
                near_copy(0, 1, j).start()

            near_copy(0, 0, j).start()

    for c in range(CYCLES):

        @pl.when(present(me + FAR_SHIFTS[c]))
        def _():
            pick_copy(c).wait_recv()
            local = pltpu.make_async_copy(pick_in.at[c], pick_sm.at[c], local_sem.at[c])
            local.start()
            local.wait()

    loads[0].wait()
    loads[1].wait()
    for j in range(AHEAD):
        send_far(2, j)

    @pl.when(present(me + 2))
    def _():
        @pl.loop(0, chunks)
        def _(j):
            fill(0, j)

            @pl.when(far_hops)
            def _():
                far_copy(3, j, hop=True).start()

    @pl.loop(0, chunks)
    def _(j):
        @pl.when(near_relays & (j < near_hop_chunks))
        def _():
            near_copy(0, 1, j, hop=True).wait_recv()
            near_on(j).start()

        @pl.when(far_relays)
        def _():
            far_copy(3, j, hop=True).wait_recv()
            far_on(j).start()

        @pl.when(j + AHEAD < chunks)
        def _():
            send_far(2, j + AHEAD)

        @pl.when(present(me + 2))
        def _():
            far_copy(0, j).start()

            @pl.when(jnp.logical_not(far_hops))
            def _():
                far_copy(3, j).start()

        send_far(1, j)
        send_near(j)

    loads[2].wait()
    scale = (1.0 / math.sqrt(HD)) * math.log2(math.e)
    extra = tile + CYCLES * FAR_ROWS
    place = lax.broadcasted_iota(jnp.int32, (1, extra), 1)
    biases = []
    for t in range(2):
        bias = jnp.where(present(me + (2 * t - 1)), 0.0, -jnp.inf)
        bias = jnp.full((1, extra), bias, jnp.float32)
        for c, shift in enumerate(FAR_SHIFTS):
            inside = place >= tile + c * FAR_ROWS
            bias = jnp.where(inside, jnp.where(present(me - shift), 0.0, -jnp.inf), bias)
        biases.append(bias)

    @pl.loop(0, chunks)
    def _(j):
        for side in range(2):

            @pl.when(present(me - (1 - 2 * side)))
            def _():
                near_copy(side, 0, j).wait_recv()
                near_copy(side, 1, j).wait_recv()

        for c in range(CYCLES):

            @pl.when(present(me - FAR_SHIFTS[c]))
            def _():
                far_copy(c, j).wait_recv()
                if c == 0:
                    far_copy(3, j).wait_recv()

        @pl.loop(0, heads)
        def _(i):
            columns = pl.ds(pl.multiple_of(j * CHUNK + i * HD, HD), HD)
            inner = pl.ds(pl.multiple_of(i * HD, HD), HD)
            own_keys = k_ref[:, columns]
            own_values = v_ref[:, columns]
            for t in range(2):
                query = q_ref[t * tile : (t + 1) * tile, columns]
                contract = (((1,), (1,)), ((), ()))
                own = lax.dot_general(query, own_keys, contract, preferred_element_type=jnp.float32)
                other = lax.dot_general(
                    query, ext[j, t, :, inner], contract, preferred_element_type=jnp.float32
                )
                other = other + biases[t]
                top = jnp.maximum(
                    jnp.max(own, axis=1, keepdims=True), jnp.max(other, axis=1, keepdims=True)
                )
                own = jnp.exp2((own - top) * scale)
                other = jnp.exp2((other - top) * scale)
                total = jnp.sum(own, axis=1, keepdims=True) + jnp.sum(other, axis=1, keepdims=True)
                mixed = jnp.dot(
                    own.astype(jnp.bfloat16), own_values, preferred_element_type=jnp.float32
                ) + jnp.dot(
                    other.astype(jnp.bfloat16), ext[j, 2 + t, :, inner],
                    preferred_element_type=jnp.float32,
                )
                o_ref[t * tile : (t + 1) * tile, columns] = (mixed / total).astype(o_ref.dtype)

    for c in range(CYCLES):

        @pl.when(present(me - FAR_SHIFTS[c]))
        def _():
            pick_copy(c).wait_send()

        @pl.when(present(me + FAR_SHIFTS[c]))
        def _():
            @pl.loop(0, chunks)
            def _(j):
                far_copy(c, j).wait_send()
                if c == 0:
                    far_copy(3, j).wait_send()

    for side in range(2):

        @pl.when(present(me + (1 - 2 * side)))
        def _():
            @pl.loop(0, chunks)
            def _(j):
                near_copy(side, 0, j).wait_send()
                near_copy(side, 1, j).wait_send()

    @pl.when(near_relays)
    def _():
        @pl.loop(0, near_hop_chunks)
        def _(j):
            near_on(j).wait_send()

    @pl.when(far_relays)
    def _():
        @pl.loop(0, chunks)
        def _(j):
            far_on(j).wait_send()


def on_device(queries, keys, values, far_pick):
    rows, width = queries.shape
    tiles = far_pick.shape[0]
    tile = rows // tiles
    chunks = width // CHUNK
    picks = jnp.pad(far_pick.reshape(1, -1), ((0, 7), (0, 128 - far_pick.size)))
    vmem = pl.BlockSpec(memory_space=pltpu.VMEM)
    hbm = pl.BlockSpec(memory_space=pltpu.HBM)
    dma = pltpu.SemaphoreType.DMA
    return pl.pallas_call(
        functools.partial(kernel, lax.axis_size("tm")),
        out_shape=jax.ShapeDtypeStruct((rows, width), queries.dtype),
        in_specs=[hbm] * 3 + [vmem],
        out_specs=vmem,
        scratch_shapes=[
            pltpu.VMEM((rows, width), queries.dtype),
            pltpu.VMEM((rows, width), keys.dtype),
            pltpu.VMEM((rows, width), values.dtype),
            pltpu.VMEM((chunks, 2 * tiles, tile + CYCLES * FAR_ROWS, CHUNK), keys.dtype),
            pltpu.VMEM((CYCLES, chunks, 2 * tiles, FAR_ROWS, CHUNK), keys.dtype),
            pltpu.VMEM((chunks, tiles, FAR_ROWS, CHUNK), values.dtype),
            pltpu.VMEM((chunks, tile, CHUNK), values.dtype),
            pltpu.VMEM((CYCLES, 8, 128), jnp.int32),
            pltpu.SMEM((CYCLES, 8, 128), jnp.int32),
            dma((4, chunks)),
            dma((4, chunks)),
            dma((CYCLES + 1, chunks)),
            dma((CYCLES + 1, chunks)),
            dma((2, chunks)),
            dma((2, chunks)),
            dma((CYCLES,)),
            dma((CYCLES,)),
            dma((CYCLES,)),
            dma((3,)),
        ],
        compiler_params=pltpu.CompilerParams(
            collective_id=0, has_side_effects=True, vmem_limit_bytes=52 * 2**20
        ),
    )(queries, keys, values, picks)


def solution(mesh):
    return jax.shard_map(
        on_device,
        mesh=mesh,
        in_specs=(
            P(("seed", "tm"), None),
            P(("seed", "tm"), None),
            P(("seed", "tm"), None),
            P("tm", None),
        ),
        out_specs=P(("seed", "tm"), None),
        check_vma=False,
    )
```

```python
import functools
import math

import jax
import jax.numpy as jnp
from jax import lax
from jax.experimental import pallas as pl
from jax.experimental.pallas import tpu as pltpu
from jax.sharding import PartitionSpec as P

HD = 128
FAR_ROWS = 64
FAR_SHIFTS = (2, -4, 8)
CYCLES = len(FAR_SHIFTS)
CHUNK = 256
AHEAD = 1
PARTNERS = (8, -8, 4, -4, 2, -2, 1, -1)


def kernel(
    n, q_hbm, k_hbm, v_hbm, pick_ref, o_ref, q_ref, k_ref, v_ref, ext, stage, far_relay, near_relay,
    pick_in, pick_sm, near_send, near_recv, far_send, far_recv, hop_recv, on_send,
    pick_send, pick_recv, local_sem, load_sem,
):
    me = lax.axis_index("tm")
    rows, width = q_ref.shape
    loads = [
        pltpu.make_async_copy(source, target, load_sem.at[i])
        for i, (source, target) in enumerate(((k_hbm, k_ref), (v_hbm, v_ref), (q_hbm, q_ref)))
    ]
    for load in loads:
        load.start()
    tile = rows // 2
    chunks = width // CHUNK
    heads = CHUNK // HD
    near_hop_chunks = chunks * 7 // 10

    def present(other):
        return (other >= 0) & (other < n)

    place4 = lax.rem(me, 4)
    far_hops = (place4 >= 2) & present(me + 2)
    far_relays = (place4 < 2) & present(me + 4)
    near_hops = (place4 == 3) & present(me + 1)
    near_relays = (place4 == 1) & present(me + 3)

    for t, step in ((0, -1), (1, 1)):

        @pl.when(jnp.logical_not(present(me + step)))
        def _():
            for j in range(chunks):
                for kv in range(2):
                    ext[j, 2 * kv + t, :tile, :] = jnp.zeros((tile, CHUNK), ext.dtype)

    for c, shift in enumerate(FAR_SHIFTS):

        @pl.when(jnp.logical_not(present(me - shift)))
        def _():
            start = tile + c * FAR_ROWS
            for j in range(chunks):
                ext[j, :, start : start + FAR_ROWS, :] = jnp.zeros((4, FAR_ROWS, CHUNK), ext.dtype)

    barrier = pltpu.get_barrier_semaphore()
    count = jnp.int32(0)
    greet = [(step, present(me + step)) for step in PARTNERS]
    greet += [(3, near_relays), (-3, (place4 == 0) & present(me - 3))]
    for step, ok in greet:
        other = me + step
        count = count + ok.astype(jnp.int32)

        @pl.when(ok)
        def _():
            pl.semaphore_signal(
                barrier, inc=1, device_id={"tm": other}, device_id_type=pl.DeviceIdType.MESH
            )

    pl.semaphore_wait(barrier, count)

    def pick_copy(c):
        return pltpu.make_async_remote_copy(
            src_ref=pick_ref, dst_ref=pick_in.at[c],
            send_sem=pick_send.at[c], recv_sem=pick_recv.at[c],
            device_id={"tm": me - FAR_SHIFTS[c]}, device_id_type=pl.DeviceIdType.MESH,
        )

    def remote(source, target, send_sem, recv_sem, step):
        return pltpu.make_async_remote_copy(
            src_ref=source, dst_ref=target, send_sem=send_sem, recv_sem=recv_sem,
            device_id={"tm": me + step}, device_id_type=pl.DeviceIdType.MESH,
        )

    def near_copy(side, kv, j, hop=False):
        source = (k_hbm, v_hbm)[kv]
        first = tile if side == 0 else 0
        columns = pl.ds(pl.multiple_of(j * CHUNK, CHUNK), CHUNK)
        source = source.at[pl.ds(first, tile), columns]
        index = 2 * side + kv
        if hop:
            return remote(source, near_relay.at[j], near_send.at[index, j], hop_recv.at[1, j], -2)
        target = ext.at[j, 2 * kv + side, pl.ds(0, tile), :]
        return remote(
            source, target, near_send.at[index, j], near_recv.at[index, j], 1 - 2 * side
        )

    def far_copy(c, j, hop=False):
        cycle, (first, count) = c % 3, {0: (0, 2), 3: (2, 2)}.get(c, (0, 4))
        source = stage.at[cycle, j, pl.ds(first, count)]
        if hop:
            return remote(source, far_relay.at[j], far_send.at[c, j], hop_recv.at[0, j], -2)
        target = ext.at[j, pl.ds(first, count), pl.ds(tile + cycle * FAR_ROWS, FAR_ROWS), :]
        return remote(source, target, far_send.at[c, j], far_recv.at[c, j], FAR_SHIFTS[cycle])

    def far_on(j):
        target = ext.at[j, pl.ds(2, 2), pl.ds(tile, FAR_ROWS), :]
        return remote(far_relay.at[j], target, on_send.at[0, j], far_recv.at[3, j], 4)

    def near_on(j):
        target = ext.at[j, 2, pl.ds(0, tile), :]
        return remote(near_relay.at[j], target, on_send.at[1, j], near_recv.at[1, j], 3)

    for c in range(CYCLES):

        @pl.when(present(me - FAR_SHIFTS[c]))
        def _():
            pick_copy(c).start()

    def send_near(j):
        @pl.when(present(me + 1) & (place4 != 3))
        def _():
            near_copy(0, 0, j).start()
            near_copy(0, 1, j).start()

        @pl.when(present(me - 1))
        def _():
            near_copy(1, 0, j).start()
            near_copy(1, 1, j).start()

    def fill(c, j):
        columns = pl.ds(pl.multiple_of(j * CHUNK, CHUNK), CHUNK)
        for t in range(2):
            pick = pick_sm[c, 0, t * CYCLES + c]
            for kv, source in enumerate((k_ref, v_ref)):
                chosen = source[:FAR_ROWS, columns]
                for p in range(1, rows // FAR_ROWS):
                    part = source[p * FAR_ROWS : (p + 1) * FAR_ROWS, columns]
                    chosen = jnp.where(pick == p, part, chosen)
                stage[c, j, 2 * kv + t] = chosen

    def send_far(c, j):
        @pl.when(present(me + FAR_SHIFTS[c]))
        def _():
            fill(c, j)
            far_copy(c, j).start()

    @pl.when(near_hops)
    def _():
        @pl.loop(0, chunks)
        def _(j):
            @pl.when(j < near_hop_chunks)
            def _():
                near_copy(0, 1, j, hop=True).start()

            @pl.when(j >= near_hop_chunks)
            def _():
                near_copy(0, 1, j).start()

            near_copy(0, 0, j).start()

    for c in range(CYCLES):

        @pl.when(present(me + FAR_SHIFTS[c]))
        def _():
            pick_copy(c).wait_recv()
            local = pltpu.make_async_copy(pick_in.at[c], pick_sm.at[c], local_sem.at[c])
            local.start()
            local.wait()

    loads[0].wait()
    loads[1].wait()
    for j in range(AHEAD):
        send_far(2, j)

    @pl.when(present(me + 2))
    def _():
        @pl.loop(0, chunks)
        def _(j):
            fill(0, j)

            @pl.when(far_hops)
            def _():
                far_copy(3, j, hop=True).start()

    @pl.loop(0, chunks)
    def _(j):
        @pl.when(near_relays & (j < near_hop_chunks))
        def _():
            near_copy(0, 1, j, hop=True).wait_recv()
            near_on(j).start()

        @pl.when(far_relays)
        def _():
            far_copy(3, j, hop=True).wait_recv()
            far_on(j).start()

        @pl.when(present(me + 2))
        def _():
            far_copy(0, j).start()

            @pl.when(jnp.logical_not(far_hops))
            def _():
                far_copy(3, j).start()

        @pl.when(j + AHEAD < chunks)
        def _():
            send_far(2, j + AHEAD)

        send_far(1, j)
        send_near(j)

    loads[2].wait()
    scale = (1.0 / math.sqrt(HD)) * math.log2(math.e)
    extra = tile + CYCLES * FAR_ROWS
    place = lax.broadcasted_iota(jnp.int32, (1, extra), 1)
    biases = []
    for t in range(2):
        bias = jnp.where(present(me + (2 * t - 1)), 0.0, -jnp.inf)
        bias = jnp.full((1, extra), bias, jnp.float32)
        for c, shift in enumerate(FAR_SHIFTS):
            inside = place >= tile + c * FAR_ROWS
            bias = jnp.where(inside, jnp.where(present(me - shift), 0.0, -jnp.inf), bias)
        biases.append(bias)

    @pl.loop(0, chunks)
    def _(j):
        for side in range(2):

            @pl.when(present(me - (1 - 2 * side)))
            def _():
                near_copy(side, 0, j).wait_recv()
                near_copy(side, 1, j).wait_recv()

        for c in range(CYCLES):

            @pl.when(present(me - FAR_SHIFTS[c]))
            def _():
                far_copy(c, j).wait_recv()
                if c == 0:
                    far_copy(3, j).wait_recv()

        @pl.loop(0, heads)
        def _(i):
            columns = pl.ds(pl.multiple_of(j * CHUNK + i * HD, HD), HD)
            inner = pl.ds(pl.multiple_of(i * HD, HD), HD)
            own_keys = k_ref[:, columns]
            own_values = v_ref[:, columns]
            for t in range(2):
                query = q_ref[t * tile : (t + 1) * tile, columns]
                contract = (((1,), (1,)), ((), ()))
                own = lax.dot_general(query, own_keys, contract, preferred_element_type=jnp.float32)
                other = lax.dot_general(
                    query, ext[j, t, :, inner], contract, preferred_element_type=jnp.float32
                )
                other = other + biases[t]
                top = jnp.maximum(
                    jnp.max(own, axis=1, keepdims=True), jnp.max(other, axis=1, keepdims=True)
                )
                own = jnp.exp2((own - top) * scale)
                other = jnp.exp2((other - top) * scale)
                total = jnp.sum(own, axis=1, keepdims=True) + jnp.sum(other, axis=1, keepdims=True)
                mixed = jnp.dot(
                    own.astype(jnp.bfloat16), own_values, preferred_element_type=jnp.float32
                ) + jnp.dot(
                    other.astype(jnp.bfloat16), ext[j, 2 + t, :, inner],
                    preferred_element_type=jnp.float32,
                )
                o_ref[t * tile : (t + 1) * tile, columns] = (mixed / total).astype(o_ref.dtype)

    for c in range(CYCLES):

        @pl.when(present(me - FAR_SHIFTS[c]))
        def _():
            pick_copy(c).wait_send()

        @pl.when(present(me + FAR_SHIFTS[c]))
        def _():
            @pl.loop(0, chunks)
            def _(j):
                far_copy(c, j).wait_send()
                if c == 0:
                    far_copy(3, j).wait_send()

    for side in range(2):

        @pl.when(present(me + (1 - 2 * side)))
        def _():
            @pl.loop(0, chunks)
            def _(j):
                near_copy(side, 0, j).wait_send()
                near_copy(side, 1, j).wait_send()

    @pl.when(near_relays)
    def _():
        @pl.loop(0, near_hop_chunks)
        def _(j):
            near_on(j).wait_send()

    @pl.when(far_relays)
    def _():
        @pl.loop(0, chunks)
        def _(j):
            far_on(j).wait_send()


def on_device(queries, keys, values, far_pick):
    rows, width = queries.shape
    tiles = far_pick.shape[0]
    tile = rows // tiles
    chunks = width // CHUNK
    picks = jnp.pad(far_pick.reshape(1, -1), ((0, 7), (0, 128 - far_pick.size)))
    vmem = pl.BlockSpec(memory_space=pltpu.VMEM)
    hbm = pl.BlockSpec(memory_space=pltpu.HBM)
    dma = pltpu.SemaphoreType.DMA
    return pl.pallas_call(
        functools.partial(kernel, lax.axis_size("tm")),
        out_shape=jax.ShapeDtypeStruct((rows, width), queries.dtype),
        in_specs=[hbm] * 3 + [vmem],
        out_specs=vmem,
        scratch_shapes=[
            pltpu.VMEM((rows, width), queries.dtype),
            pltpu.VMEM((rows, width), keys.dtype),
            pltpu.VMEM((rows, width), values.dtype),
            pltpu.VMEM((chunks, 2 * tiles, tile + CYCLES * FAR_ROWS, CHUNK), keys.dtype),
            pltpu.VMEM((CYCLES, chunks, 2 * tiles, FAR_ROWS, CHUNK), keys.dtype),
            pltpu.VMEM((chunks, tiles, FAR_ROWS, CHUNK), values.dtype),
            pltpu.VMEM((chunks, tile, CHUNK), values.dtype),
            pltpu.VMEM((CYCLES, 8, 128), jnp.int32),
            pltpu.SMEM((CYCLES, 8, 128), jnp.int32),
            dma((4, chunks)),
            dma((4, chunks)),
            dma((CYCLES + 1, chunks)),
            dma((CYCLES + 1, chunks)),
            dma((2, chunks)),
            dma((2, chunks)),
            dma((CYCLES,)),
            dma((CYCLES,)),
            dma((CYCLES,)),
            dma((3,)),
        ],
        compiler_params=pltpu.CompilerParams(
            collective_id=0, has_side_effects=True, vmem_limit_bytes=52 * 2**20
        ),
    )(queries, keys, values, picks)


def solution(mesh):
    return jax.shard_map(
        on_device,
        mesh=mesh,
        in_specs=(
            P(("seed", "tm"), None),
            P(("seed", "tm"), None),
            P(("seed", "tm"), None),
            P("tm", None),
        ),
        out_specs=P(("seed", "tm"), None),
        check_vma=False,
    )
```
